128 devices in a mesh: frames: 16 (over x_hi, y, core), rows: 8 (over x_lo, z).
Axes of the slice: x: 4 (x_hi: 2, x_lo: 2; x = x_hi * 2 + x_lo), y: 4, z: 4, core: 2. Of those that a mesh axis runs over, the one named last changes fastest.
Arguments:
- clip: bfloat16 [32, 64, 512, 256], P('frames', 'rows'), may hold values from -6 to 6
- w_query: bfloat16 [256, 256], replicated, may hold values from -32 to 32
- w_key: bfloat16 [256, 256], replicated, may hold values from -1 to 1
- w_value: bfloat16 [256, 256], replicated, may hold values from -0.375 to 0.375
- w_out: bfloat16 [256, 256], replicated, may hold values from -0.375 to 0.375
- w_conv: bfloat16 [3, 3, 256, 256], replicated, may hold values from -0.125 to 0.125
- conv_bias: float32 [256], replicated, may hold values from -3 to 3
Outputs:
- upsampled: bfloat16 [32, 128, 512, 128], P('frames', 'rows')
The draws below stay inside these ranges and needn't reach their ends.
All inputs are finite; a program needn't handle non-finite values.
Results may differ from the reference program's by a relative error of at most 0.012.
Values may be sent and summed in bfloat16 or wider, within the bound.
No kernel may reach another device: no remote copies, remote signals or barrier semaphores. Data moves between devices by JAX's collectives and lax.ppermute only.
A program may use at most 192 MiB of HBM per device.

```python
import math
import jax
import jax.numpy as jnp
from jax import lax

C = 256
HEADS = 8
HD = 32
CO = 64
W = 512
FRAMES = 32
H = 64


def key_matrix(key):
    return jax.random.normal(key, (C, C), jnp.float32) / math.sqrt(C)


def draw_w_key(key, part):
    return jnp.clip(key_matrix(key), -1.0, 1.0).astype(jnp.bfloat16)


def draw_w_query(key, part):
    key = jax.random.fold_in(key, 7)
    own = jnp.clip(jax.random.normal(key, (C, C), jnp.float32) / math.sqrt(C), -1.0, 1.0)
    matrix = own
    return matrix.astype(jnp.bfloat16)


def draw_clip(key, part):
    key = jax.random.fold_in(key, 11)
    values = jax.random.normal(key, (FRAMES, H, W, C), jnp.float32)
    return jnp.clip(values, -6.0, 6.0).astype(jnp.bfloat16)


def scatter_about(stream_key, extent, scale, reach, held_as=jnp.bfloat16):
    values = scale * jax.random.normal(stream_key, extent, jnp.float32)
    return jnp.clip(values, min=-reach, max=reach).astype(held_as)


def setup_inputs(seed: int = 0) -> dict:
    seeds = jax.random.split(jax.random.key(seed), 8)
    clip = draw_clip(jax.random.fold_in(seeds[7], 71), 0)
    w_query = draw_w_query(jax.random.fold_in(seeds[7], 71), 0)
    w_key = draw_w_key(jax.random.fold_in(seeds[7], 71), 0)
    w_value = scatter_about(seeds[3], (C, C), C ** -0.5, 0.375)
    w_out = scatter_about(seeds[4], (C, C), C ** -0.5, 0.375)
    w_conv = scatter_about(seeds[5], (3, 3, C, C), (9 * C) ** -0.5, 0.125)
    conv_bias = scatter_about(seeds[6], (C,), 0.5, 3.0, jnp.float32)
    return {"clip": clip, "w_query": w_query, "w_key": w_key, "w_value": w_value, "w_out": w_out, "w_conv": w_conv, "conv_bias": conv_bias}


def normalize(x):
    values = x.astype(jnp.float32)
    mean = lax.optimization_barrier(jnp.mean(values, axis=-1, keepdims=True))
    centred = values - mean
    var = lax.optimization_barrier(jnp.mean(centred * centred, axis=-1, keepdims=True))
    return (centred * lax.rsqrt(var + 1e-06)).astype(jnp.bfloat16)

def project(x, weight):
    shape = x.shape
    out = jnp.dot(x.reshape(-1, shape[-1]), weight, preferred_element_type=jnp.float32)
    return out.astype(jnp.bfloat16).reshape(shape[:-1] + (weight.shape[1],))

def one_row(row, w_query, w_key, w_value, w_out):
    frames_all, width, chans = row.shape
    normed = normalize(row)
    query = project(normed, w_query).reshape(frames_all, width, HEADS, HD)
    keys = project(normed, w_key).reshape(frames_all, width, HEADS, HD)
    values = project(normed, w_value).reshape(frames_all, width, HEADS, HD)
    scores = jnp.einsum('fphd,gphd->phfg', query.astype(jnp.float32), keys.astype(jnp.float32)) / jnp.sqrt(jnp.float32(HD))
    probs = jax.nn.softmax(scores, axis=-1).astype(jnp.bfloat16)
    attended = jnp.einsum('phfg,gphd->fphd', probs.astype(jnp.float32), values.astype(jnp.float32)).astype(jnp.bfloat16)
    return project(attended.reshape(frames_all, width, chans), w_out)

def reference(clip, w_query, w_key, w_value, w_out, w_conv, conv_bias):
    by_rows = jnp.moveaxis(clip, 1, 0)
    projected = lax.map(lambda row: one_row(row, w_query, w_key, w_value, w_out), by_rows)
    projected = jnp.moveaxis(projected, 0, 1)
    hidden = clip.astype(jnp.float32) + projected.astype(jnp.float32)
    activated = jax.nn.silu(hidden).astype(jnp.bfloat16)
    convolved = lax.conv_general_dilated(activated, w_conv, (1, 1), ((1, 1), (1, 1)), dimension_numbers=('NHWC', 'HWIO', 'NHWC'), preferred_element_type=jnp.float32)
    mixed = (hidden + convolved + conv_bias).astype(jnp.bfloat16)
    frames_all, height, width, chans = mixed.shape
    split = mixed.reshape(frames_all, height, width, 2, 2 * CO)
    return jnp.transpose(split, (0, 1, 3, 2, 4)).reshape(frames_all, 2 * height, width, 2 * CO)
```

```python
import jax
import jax.numpy as jnp
import numpy as np
from jax import lax
from jax.experimental import pallas as pl
from jax.experimental.pallas import tpu as pltpu
from jax.sharding import PartitionSpec as P

HEADS = 8
HEAD = 32
FRAMES = 32
C = 256
GROUP = 8
F32 = jnp.float32
BF16 = jnp.bfloat16


def dot(a, b):
    return jnp.dot(a, b, preferred_element_type=F32)


def dot_nt(a, b):
    return lax.dot_general(a, b, (((1,), (1,)), ((), ())), preferred_element_type=F32)


def group_max(s):
    halves = []
    for i in range(s.shape[1] // 128):
        m = s[:, 128 * i : 128 * (i + 1)]
        lanes = lax.broadcasted_iota(jnp.int32, m.shape, 1)
        for step in (1, 2, 4, 8, 16):
            m = jnp.maximum(m, jnp.take_along_axis(m, lanes ^ step, axis=1))
        halves.append(m)
    return jnp.concatenate(halves, axis=1)


def attention_kernel(x_ref, wq_ref, wk_ref, wv_ref, wo_ref, perm_ref, back_ref, same_ref, out_ref):
    pixels = x_ref.shape[1]
    x = x_ref[...].astype(F32)
    mean = jnp.mean(x, axis=-1, keepdims=True)
    centred = x - mean
    var = jnp.mean(centred * centred, axis=-1, keepdims=True)
    normed = centred * lax.rsqrt(var + 1e-6)
    rows = GROUP * FRAMES
    parts = []
    for j in range(pixels // GROUP):
        part = normed[:, j * GROUP : (j + 1) * GROUP].reshape(rows, C).astype(BF16)
        parts.append(dot(perm_ref[...], part).astype(BF16))
    xp = jnp.concatenate(parts, axis=0)
    q = dot(xp, wq_ref[...]).astype(BF16)
    k = dot(xp, wk_ref[...]).astype(BF16)
    v = dot(xp, wv_ref[...]).astype(BF16)
    same = same_ref[...]
    scores = []
    for p in range(pixels):
        at = slice(p * FRAMES, (p + 1) * FRAMES)
        scores.append(dot_nt(q[at], jnp.concatenate([k[at]] * HEADS, axis=0) * same))
    s = jnp.concatenate(scores, axis=0)
    factor = np.float32(np.log2(np.e) / np.sqrt(HEAD))
    e = jnp.exp2((s - group_max(s)) * factor).astype(BF16)
    total = dot(e, same)
    sums = []
    for p in range(pixels):
        at = slice(p * FRAMES, (p + 1) * FRAMES)
        sums.append(dot(e[at], jnp.concatenate([v[at]] * HEADS, axis=0) * same))
    attended = (jnp.concatenate(sums, axis=0) / total).astype(BF16)
    projected = dot(attended, wo_ref[...]).astype(BF16)
    for j in range(pixels // GROUP):
        part = dot(back_ref[...], projected[j * rows : (j + 1) * rows])
        parts[j] = part.reshape(FRAMES, GROUP, C)
    out_ref[...] = jnp.concatenate(parts, axis=1).astype(BF16)


def attention(x, wq, wk, wv, wo, pixels=16):
    count = x.shape[1]
    row = np.arange(GROUP * FRAMES)
    source = (row % FRAMES) * GROUP + row // FRAMES
    perm = (source[:, None] == row[None, :]).astype(np.float32)
    same = (row[:, None] // HEAD == row[None, :] // HEAD).astype(np.float32)
    whole = pl.BlockSpec((C, C), lambda i: (0, 0))
    block = pl.BlockSpec((FRAMES, pixels, C), lambda i: (0, i, 0))
    tokens = FRAMES * count
    return pl.pallas_call(
        attention_kernel,
        out_shape=jax.ShapeDtypeStruct(x.shape, BF16),
        grid=(count // pixels,),
        in_specs=[block] + [whole] * 7,
        out_specs=block,
        compiler_params=pltpu.CompilerParams(vmem_limit_bytes=48 * 2**20),
        cost_estimate=pl.CostEstimate(
            flops=2 * tokens * C * C * 8, bytes_accessed=4 * tokens * C, transcendentals=tokens * C
        ),
        name="attention",
    )(x, wq, wk, wv, wo, jnp.asarray(perm, BF16), jnp.asarray(perm.T, BF16), jnp.asarray(same, BF16))


def silu(v):
    return v / (1.0 + jnp.exp(-v))


def conv_kernel(clip_ref, proj_ref, up_ref, down_ref, w_ref, bias_ref, out_ref, act_ref, hid_ref):
    rows, width = clip_ref.shape[1], clip_ref.shape[2]
    pix = lax.broadcasted_iota(jnp.int32, (width, C), 0)

    def put(row, act):
        before = jnp.where(pix == 0, 0.0, pltpu.roll(act, 1, 0))
        after = jnp.where(pix == width - 1, 0.0, pltpu.roll(act, width - 1, 0))
        act_ref[row, :, 0:C] = before.astype(BF16)
        act_ref[row, :, C : 2 * C] = act.astype(BF16)
        act_ref[row, :, 2 * C :] = after.astype(BF16)

    def load(r):
        p = jnp.concatenate([proj_ref[2 * r, 0], proj_ref[2 * r + 1, 0]], axis=0)
        hidden = clip_ref[0, r].astype(F32) + p.astype(F32)
        hid_ref[r % 2] = hidden
        put(r + 1, silu(hidden).astype(BF16).astype(F32))

    put(0, up_ref[0, 0].astype(F32))
    load(0)
    for r in range(rows):
        if r + 1 < rows:
            load(r + 1)
        else:
            put(rows + 1, down_ref[0, 0].astype(F32))
        acc = hid_ref[r % 2] + bias_ref[...]
        for dy in range(3):
            acc = acc + dot(act_ref[r + dy], w_ref[dy])
        mixed = acc.astype(BF16)
        out_ref[0, 2 * r] = mixed[:, : C // 2]
        out_ref[0, 2 * r + 1] = mixed[:, C // 2 :]


def conv(clip, proj, up, down, w, bias):
    frames, rows, width, _ = clip.shape
    return pl.pallas_call(
        conv_kernel,
        out_shape=jax.ShapeDtypeStruct((frames, 2 * rows, width, C // 2), BF16),
        grid=(frames,),
        in_specs=[
            pl.BlockSpec((1, rows, width, C), lambda f: (f, 0, 0, 0)),
            pl.BlockSpec((2 * rows, 1, width // 2, C), lambda f: (0, f, 0, 0)),
            pl.BlockSpec((1, 1, width, C), lambda f: (f, 0, 0, 0)),
            pl.BlockSpec((1, 1, width, C), lambda f: (f, 0, 0, 0)),
            pl.BlockSpec((3, 3 * C, C), lambda f: (0, 0, 0)),
            pl.BlockSpec((1, C), lambda f: (0, 0)),
        ],
        out_specs=pl.BlockSpec((1, 2 * rows, width, C // 2), lambda f: (f, 0, 0, 0)),
        scratch_shapes=[
            pltpu.VMEM((rows + 2, width, 3 * C), BF16),
            pltpu.VMEM((2, width, C), F32),
        ],
        compiler_params=pltpu.CompilerParams(vmem_limit_bytes=56 * 2**20),
        cost_estimate=pl.CostEstimate(
            flops=2 * frames * rows * width * 9 * C * C,
            bytes_accessed=6 * frames * rows * width * C,
            transcendentals=frames * rows * width * C,
        ),
        name="residual_conv",
    )(clip, proj, up, down, w.reshape(3, 3 * C, C), bias.reshape(1, C))


def local(clip, w_query, w_key, w_value, w_out, w_conv, conv_bias):
    frames, rows, width, chans = clip.shape
    n = lax.axis_size("frames")
    share = rows * width // n
    cut = clip.reshape(frames, n, share, chans).transpose(1, 0, 2, 3)
    got = lax.all_to_all(cut, "frames", split_axis=0, concat_axis=0, tiled=True)
    proj = attention(got.reshape(n * frames, share, chans), w_query, w_key, w_value, w_out)
    proj = proj.reshape(n, frames, share, chans)
    proj = lax.all_to_all(proj, "frames", split_axis=0, concat_axis=0, tiled=True)
    per = width // share

    def edge(r):
        p = proj[r * per : (r + 1) * per].transpose(1, 0, 2, 3).reshape(frames, 1, width, chans)
        hidden = clip[:, r : r + 1].astype(F32) + p.astype(F32)
        return silu(hidden).astype(BF16)

    size = lax.axis_size("rows")
    up = lax.ppermute(edge(rows - 1), "rows", [(i, i + 1) for i in range(size - 1)])
    down = lax.ppermute(edge(0), "rows", [(i + 1, i) for i in range(size - 1)])
    return conv(clip, proj, up, down, w_conv, conv_bias)


def solution(mesh):
    placed = (P("frames", "rows", None, None), P(), P(), P(), P(), P(), P())
    return jax.shard_map(
        local,
        mesh=mesh,
        in_specs=placed,
        out_specs=P("frames", "rows", None, None),
        check_vma=False,
    )
```

```python
import functools

import jax
import jax.numpy as jnp
import numpy as np
from jax import lax
from jax.experimental import pallas as pl
from jax.experimental.pallas import tpu as pltpu
from jax.sharding import PartitionSpec as P

HEADS = 8
HEAD = 32
FRAMES = 32
C = 256
GROUP = 8
VMEM = 60 * 2**20
F32 = jnp.float32
BF16 = jnp.bfloat16


def dot(a, b):
    return jnp.dot(a, b, preferred_element_type=F32)


def dot_nt(a, b):
    return lax.dot_general(a, b, (((1,), (1,)), ((), ())), preferred_element_type=F32)


def group_max(s):
    t = s.T
    rows = t.shape[1]
    m = jnp.max(t.reshape(HEADS, HEAD, rows), axis=1, keepdims=True)
    return jnp.broadcast_to(m, (HEADS, HEAD, rows)).reshape(C, rows).T


def attention_kernel(parts_in, slots_ref, *refs):
    x_refs = refs[:parts_in]
    wq_ref, wk_ref, wv_ref, wo_ref, perm_ref, back_ref, same_ref = refs[parts_in : parts_in + 7]
    out_ref = refs[-1]
    pixels = x_refs[0].shape[-2]
    x = jnp.concatenate([r[...].reshape(-1, pixels, C) for r in x_refs], axis=0).astype(F32)
    mean = jnp.mean(x, axis=-1, keepdims=True)
    centred = x - mean
    var = jnp.mean(centred * centred, axis=-1, keepdims=True)
    normed = centred * lax.rsqrt(var + 1e-6)
    rows = GROUP * FRAMES
    parts = []
    for j in range(pixels // GROUP):
        part = normed[:, j * GROUP : (j + 1) * GROUP].reshape(rows, C).astype(BF16)
        parts.append(dot(perm_ref[...], part).astype(BF16))
    xp = jnp.concatenate(parts, axis=0)
    q = dot(xp, wq_ref[...]).astype(BF16)
    k = dot(xp, wk_ref[...]).astype(BF16)
    v = dot(xp, wv_ref[...]).astype(BF16)
    same = same_ref[...]
    scores = []
    for p in range(pixels):
        at = slice(p * FRAMES, (p + 1) * FRAMES)
        scores.append(dot_nt(q[at], jnp.concatenate([k[at]] * HEADS, axis=0) * same))
    s = jnp.concatenate(scores, axis=0)
    factor = np.float32(np.log2(np.e) / np.sqrt(HEAD))
    e = jnp.exp2((s - group_max(s)) * factor).astype(BF16)
    total = dot(e, same)
    sums = []
    for p in range(pixels):
        at = slice(p * FRAMES, (p + 1) * FRAMES)
        sums.append(dot(e[at], jnp.concatenate([v[at]] * HEADS, axis=0) * same))
    attended = (jnp.concatenate(sums, axis=0) / total).astype(BF16)
    projected = dot(attended, wo_ref[...]).astype(BF16)
    for j in range(pixels // GROUP):
        part = dot(back_ref[...], projected[j * rows : (j + 1) * rows])
        parts[j] = part.reshape(FRAMES, GROUP, C)
    out = jnp.concatenate(parts, axis=1).astype(BF16)
    for i in range(FRAMES // 2):
        out_ref[slots_ref[i]] = out[2 * i : 2 * i + 2]


def attention(slots, xs, weights, pixels, cost):
    count = xs[0].shape[-2]
    row = np.arange(GROUP * FRAMES)
    source = (row % FRAMES) * GROUP + row // FRAMES
    perm = (source[:, None] == row[None, :]).astype(np.float32)
    same = (row[:, None] // HEAD == row[None, :] // HEAD).astype(np.float32)
    whole = pl.BlockSpec((C, C), lambda i, s: (0, 0))
    blocks = []
    for x in xs:
        if x.ndim == 3:
            blocks.append(pl.BlockSpec((x.shape[0], pixels, C), lambda i, s: (0, i, 0)))
        else:
            shape = (x.shape[0], 1, x.shape[2], pixels, C)
            blocks.append(pl.BlockSpec(shape, lambda i, s: (0, s[FRAMES // 2], 0, i, 0)))
    pairs = FRAMES // 2
    return pl.pallas_call(
        functools.partial(attention_kernel, len(xs)),
        out_shape=jax.ShapeDtypeStruct((pairs, 2, count, C), BF16),
        grid_spec=pltpu.PrefetchScalarGridSpec(
            num_scalar_prefetch=1,
            grid=(count // pixels,),
            in_specs=blocks + [whole] * 7,
            out_specs=pl.BlockSpec((pairs, 2, pixels, C), lambda i, s: (0, 0, i, 0)),
        ),
        compiler_params=pltpu.CompilerParams(vmem_limit_bytes=VMEM),
        cost_estimate=pl.CostEstimate(flops=cost, bytes_accessed=cost // 1000, transcendentals=0),
        name="attention",
    )(slots, *xs, *weights, jnp.asarray(perm, BF16), jnp.asarray(perm.T, BF16), jnp.asarray(same, BF16))


def silu(v):
    return v / (1.0 + jnp.exp(-v))


EARLY = (0, 3)
LATE = (1, 2)


def hidden_row(clip_refs, proj_ref, i):
    p = jnp.concatenate([proj_ref[4 * i + j, 0] for j in range(4)], axis=0)
    return clip_refs[i // 2][0, i % 2].astype(F32) + p.astype(F32)


def put(act_ref, slot, act):
    width = act.shape[0]
    pix = lax.broadcasted_iota(jnp.int32, act.shape, 0)
    before = jnp.where(pix == 0, 0.0, pltpu.roll(act, 1, 0))
    after = jnp.where(pix == width - 1, 0.0, pltpu.roll(act, width - 1, 0))
    act_ref[slot, :, 0:C] = before.astype(BF16)
    act_ref[slot, :, C : 2 * C] = act.astype(BF16)
    act_ref[slot, :, 2 * C :] = after.astype(BF16)


def activate(hidden):
    return silu(hidden).astype(BF16).astype(F32)


def early_kernel(top_ref, bottom_ref, proj_ref, w_ref, bias_ref, part_ref, last_ref, lead_ref, act_ref):
    bias = bias_ref[...]

    def load(i):
        hidden = hidden_row((top_ref, bottom_ref), proj_ref, i)
        put(act_ref, i, activate(hidden))
        return hidden + bias

    first = load(0)
    second = load(1)
    part_ref[0, 0] = first + dot(act_ref[0], w_ref[1]) + dot(act_ref[1], w_ref[2])
    sixth = load(2)
    part_ref[0, 1] = second + dot(act_ref[0], w_ref[0]) + dot(act_ref[1], w_ref[1])
    part_ref[0, 2] = dot(act_ref[1], w_ref[0])
    seventh = load(3)
    part_ref[0, 3] = dot(act_ref[2], w_ref[2])
    part_ref[0, 4] = sixth + dot(act_ref[2], w_ref[1]) + dot(act_ref[3], w_ref[2])
    part_ref[0, 5] = seventh + dot(act_ref[2], w_ref[0]) + dot(act_ref[3], w_ref[1])
    last_ref[0, 0] = act_ref[3, :, C : 2 * C]
    lead_ref[0, 0] = act_ref[0, :, C : 2 * C]


def late_kernel(top_ref, bottom_ref, proj_ref, up_ref, down_ref, part_ref, w_ref, bias_ref, out_ref, act_ref, hid_ref):
    bias = bias_ref[...]

    def load(i):
        hidden = hidden_row((top_ref, bottom_ref), proj_ref, i)
        hid_ref[i] = hidden + bias
        put(act_ref, i, activate(hidden))

    def finish(row, acc):
        mixed = acc.astype(BF16)
        out_ref[0, 2 * row] = mixed[:, : C // 2]
        out_ref[0, 2 * row + 1] = mixed[:, C // 2 :]

    put(act_ref, 4, up_ref[0, 0].astype(F32))
    load(0)
    finish(0, part_ref[0, 0] + dot(act_ref[4], w_ref[0]))
    load(1)
    finish(1, part_ref[0, 1] + dot(act_ref[0], w_ref[2]))
    load(2)
    finish(2, part_ref[0, 2] + hid_ref[0] + dot(act_ref[0], w_ref[1]) + dot(act_ref[1], w_ref[2]))
    load(3)
    for row in (3, 4):
        acc = hid_ref[row - 2]
        for dy in range(3):
            acc = acc + dot(act_ref[row - 3 + dy], w_ref[dy])
        finish(row, acc)
    put(act_ref, 5, down_ref[0, 0].astype(F32))
    finish(5, part_ref[0, 3] + hid_ref[3] + dot(act_ref[2], w_ref[0]) + dot(act_ref[3], w_ref[1]))
    finish(6, part_ref[0, 4] + dot(act_ref[3], w_ref[0]))
    finish(7, part_ref[0, 5] + dot(act_ref[5], w_ref[2]))


def row_pair(clip, i):
    return pl.BlockSpec((1, 2) + clip.shape[2:], lambda f: (f, i, 0, 0))


def per_frame(shape):
    zeros = (0,) * (len(shape) - 1)
    return pl.BlockSpec((1,) + shape[1:], lambda f: (f,) + zeros)


def conv_specs(width, places, share):
    return (
        pl.BlockSpec((places, 1, share, C), lambda f: (0, f, 0, 0)),
        pl.BlockSpec((3, 3 * C, C), lambda f: (0, 0, 0)),
        pl.BlockSpec((1, C), lambda f: (0, 0)),
    )


def cost(frames, rows, width):
    return pl.CostEstimate(
        flops=2 * frames * rows * width * 9 * C * C,
        bytes_accessed=8 * frames * rows * width * C,
        transcendentals=frames * rows * width * C,
    )


def conv_early(clip, proj, w, bias):
    frames, rows, width, _ = clip.shape
    proj_spec, w_spec, bias_spec = conv_specs(width, proj.shape[0], proj.shape[2])
    edge = jax.ShapeDtypeStruct((frames, 1, width, C), BF16)
    outs = (jax.ShapeDtypeStruct((frames, 6, width, C), F32), edge, edge)
    return pl.pallas_call(
        early_kernel,
        out_shape=outs,
        grid=(frames,),
        in_specs=[row_pair(clip, EARLY[0]), row_pair(clip, EARLY[1]), proj_spec, w_spec, bias_spec],
        out_specs=tuple(per_frame(o.shape) for o in outs),
        scratch_shapes=[pltpu.VMEM((4, width, 3 * C), BF16)],
        compiler_params=pltpu.CompilerParams(vmem_limit_bytes=VMEM),
        cost_estimate=cost(frames, 4, width),
        name="conv_early",
    )(clip, clip, proj, w, bias)


def conv_late(clip, proj, up, down, part, w, bias):
    frames, rows, width, _ = clip.shape
    proj_spec, w_spec, bias_spec = conv_specs(width, proj.shape[0], proj.shape[2])
    out = jax.ShapeDtypeStruct((frames, 2 * rows, width, C // 2), BF16)
    return pl.pallas_call(
        late_kernel,
        out_shape=out,
        grid=(frames,),
        in_specs=[
            row_pair(clip, LATE[0]),
            row_pair(clip, LATE[1]),
            proj_spec,
            per_frame(up.shape),
            per_frame(down.shape),
            per_frame(part.shape),
            w_spec,
            bias_spec,
        ],
        out_specs=per_frame(out.shape),
        scratch_shapes=[pltpu.VMEM((6, width, 3 * C), BF16), pltpu.VMEM((4, width, C), F32)],
        compiler_params=pltpu.CompilerParams(vmem_limit_bytes=VMEM),
        cost_estimate=cost(frames, 4, width),
        name="conv_late",
    )(clip, clip, proj, up, down, part, w, bias)


def early_cut_kernel(clip_ref, out_ref):
    for f in range(out_ref.shape[2]):
        out_ref[:, :, f] = clip_ref[f]


def early_cut(clip, owners):
    frames, rows, width, _ = clip.shape
    share = 4 * width // owners
    runs = width // share
    return pl.pallas_call(
        early_cut_kernel,
        out_shape=jax.ShapeDtypeStruct((4, runs, frames, share, C), BF16),
        grid=(2,),
        in_specs=[pl.BlockSpec((frames, 2, runs, share, C), lambda i: (0, EARLY[1] * i, 0, 0, 0))],
        out_specs=pl.BlockSpec((2, runs, frames, share, C), lambda i: (i, 0, 0, 0, 0)),
        compiler_params=pltpu.CompilerParams(vmem_limit_bytes=VMEM),
        cost_estimate=pl.CostEstimate(flops=1000, bytes_accessed=1000, transcendentals=0),
        name="early_cut",
    )(clip.reshape(frames, rows, runs, share, C)).reshape(owners, frames, share, C)


def late_cut_kernel(half_ref, near_ref, far_ref, mine_ref, away_ref):
    mine_ref[:, :, 0] = near_ref[0]
    away_ref[:, :, 0] = far_ref[0]


def late_cut(half, clip, owners):
    frames, rows, width, _ = clip.shape
    share = 4 * width // owners
    runs = width // share
    out = jax.ShapeDtypeStruct((2, runs, frames, share, C), BF16)
    block = (1, 2, runs, share, C)
    out_spec = pl.BlockSpec((2, runs, 1, share, C), lambda f, s: (0, 0, f, 0, 0))
    clip = clip.reshape(frames, rows, runs, share, C)
    outs = pl.pallas_call(
        late_cut_kernel,
        out_shape=(out, out),
        grid_spec=pltpu.PrefetchScalarGridSpec(
            num_scalar_prefetch=1,
            grid=(frames,),
            in_specs=[
                pl.BlockSpec(block, lambda f, s: (f, LATE[0] + s[0], 0, 0, 0)),
                pl.BlockSpec(block, lambda f, s: (f, LATE[1] - s[0], 0, 0, 0)),
            ],
            out_specs=(out_spec, out_spec),
        ),
        compiler_params=pltpu.CompilerParams(vmem_limit_bytes=VMEM),
        cost_estimate=pl.CostEstimate(flops=1000, bytes_accessed=1000, transcendentals=0),
        name="late_cut",
    )(half, clip, clip)
    return [o.reshape(owners // 4, 2, frames, share, C) for o in outs]


CHIPS = 8


def exchange(a):
    return lax.all_to_all(a, "frames", split_axis=0, concat_axis=0, tiled=True)


def to_chip(a, k):
    pairs = []
    for i in range(2 * CHIPS):
        x, y, core = i // 8, i // 2 % 4, i % 2
        pairs.append((i, ((x + core) % 2 * 4 + (y + k) % 4) * 2 + core))
    return lax.ppermute(a, "frames", pairs)


def to_sibling(a):
    return lax.ppermute(a, "frames", [(i, i ^ 1) for i in range(2 * CHIPS)])


def pick(a, i, axis=0):
    return lax.dynamic_index_in_dim(a, i, axis, keepdims=False)


def local(clip, w_query, w_key, w_value, w_out, w_conv, conv_bias):
    weights = (w_query, w_key, w_value, w_out)
    frames, rows, width, chans = clip.shape
    me = lax.axis_index("frames")
    x, y, core = me // 8, me // 2 % 4, me % 2
    other = 1 - core
    w = w_conv.reshape(3, 3 * C, C)
    bias = conv_bias.reshape(1, C)

    early, clip_late = lax.optimization_barrier((early_cut(clip, 2 * CHIPS), clip))
    early = exchange(early)
    share = early.shape[2]
    early = early.reshape(FRAMES, share, chans)

    mine, away = late_cut(((x + core) % 2).astype(jnp.int32).reshape(1), clip_late, 2 * CHIPS)
    theirs = to_sibling(away)
    got = []
    for k in range(4):
        to = (y + k) % 4
        got.append(to_chip(jnp.stack([pick(mine, to), pick(theirs, to)]), k))

    order = jnp.arange(2 * CHIPS + 1, dtype=jnp.int32)
    proj = attention(order, [early], weights, 64, 1000)
    proj_early = exchange(proj)
    _, *got = lax.optimization_barrier((proj, *got))

    give = jnp.stack([pick(g, other, 1) for g in got]).reshape(FRAMES // 2, share, chans)
    theirs = to_sibling(give)
    slots = []
    for c in (core, other):
        for k in range(4):
            for s in range(2):
                slots.append(((x + c) % 2 * 4 + (y + 4 - k) % 4) * 2 + (c + s) % 2)
    slots = jnp.stack(slots + [core]).astype(jnp.int32)
    proj_late = exchange(attention(slots, [*got, theirs], weights, 64, 5 * 10**9))

    part, last, lead = conv_early(clip, proj_early, w, bias)
    size = lax.axis_size("rows")
    up = lax.ppermute(last, "rows", [(i, i + 1) for i in range(size - 1)])
    down = lax.ppermute(lead, "rows", [(i + 1, i) for i in range(size - 1)])
    return conv_late(clip, proj_late, up, down, part, w, bias)


def solution(mesh):
    placed = (P("frames", "rows", None, None), P(), P(), P(), P(), P(), P())
    return jax.shard_map(
        local,
        mesh=mesh,
        in_specs=placed,
        out_specs=P("frames", "rows", None, None),
        check_vma=False,
    )
```

```python
import functools

import jax
import jax.numpy as jnp
import numpy as np
from jax import lax
from jax.experimental import pallas as pl
from jax.experimental.pallas import tpu as pltpu
from jax.sharding import PartitionSpec as P

HEADS = 8
HEAD = 32
FRAMES = 32
C = 256
GROUP = 8
VMEM = 63 * 2**20
F32 = jnp.float32
BF16 = jnp.bfloat16


def dot(a, b):
    return jnp.dot(a, b, preferred_element_type=F32)


def dot_nt(a, b):
    return lax.dot_general(a, b, (((1,), (1,)), ((), ())), preferred_element_type=F32)


def group_max(s):
    t = s.T
    rows = t.shape[1]
    m = jnp.max(t.reshape(HEADS, HEAD, rows), axis=1, keepdims=True)
    return jnp.broadcast_to(m, (HEADS, HEAD, rows)).reshape(C, rows).T


def attention_kernel(parts_in, ordered, *refs):
    slots_ref, refs = (range(FRAMES // 2), refs) if ordered else (refs[0], refs[1:])
    x_refs = refs[:parts_in]
    wq_ref, wk_ref, wv_ref, wo_ref, perm_ref, back_ref, same_ref = refs[parts_in : parts_in + 7]
    out_ref = refs[-1]
    pixels = x_refs[0].shape[-2]
    x = jnp.concatenate([r[...].reshape(-1, pixels, C) for r in x_refs], axis=0).astype(F32)
    mean = jnp.mean(x, axis=-1, keepdims=True)
    centred = x - mean
    var = jnp.mean(centred * centred, axis=-1, keepdims=True)
    normed = centred * lax.rsqrt(var + 1e-6)
    rows = GROUP * FRAMES
    parts = []
    for j in range(pixels // GROUP):
        part = normed[:, j * GROUP : (j + 1) * GROUP].reshape(rows, C).astype(BF16)
        parts.append(dot(perm_ref[...], part).astype(BF16))
    xp = jnp.concatenate(parts, axis=0)
    q = dot(xp, wq_ref[...]).astype(BF16)
    k = dot(xp, wk_ref[...]).astype(BF16)
    v = dot(xp, wv_ref[...]).astype(BF16)
    same = same_ref[...]
    scores = []
    for p in range(pixels):
        at = slice(p * FRAMES, (p + 1) * FRAMES)
        scores.append(dot_nt(q[at], jnp.concatenate([k[at]] * HEADS, axis=0) * same))
    s = jnp.concatenate(scores, axis=0)
    factor = np.float32(np.log2(np.e) / np.sqrt(HEAD))
    e = jnp.exp2((s - group_max(s)) * factor).astype(BF16)
    total = dot(e, same)
    sums = []
    for p in range(pixels):
        at = slice(p * FRAMES, (p + 1) * FRAMES)
        sums.append(dot(e[at], jnp.concatenate([v[at]] * HEADS, axis=0) * same))
    attended = (jnp.concatenate(sums, axis=0) / total).astype(BF16)
    projected = dot(attended, wo_ref[...]).astype(BF16)
    for j in range(pixels // GROUP):
        part = dot(back_ref[...], projected[j * rows : (j + 1) * rows])
        parts[j] = part.reshape(FRAMES, GROUP, C)
    out = jnp.concatenate(parts, axis=1).astype(BF16)
    for i in range(FRAMES // 2):
        out_ref[slots_ref[i]] = out[2 * i : 2 * i + 2]


def attention(slots, xs, weights, pixels, cost):
    slots = [] if slots is None else [slots]
    count = xs[0].shape[-2]
    row = np.arange(GROUP * FRAMES)
    source = (row % FRAMES) * GROUP + row // FRAMES
    perm = (source[:, None] == row[None, :]).astype(np.float32)
    same = (row[:, None] // HEAD == row[None, :] // HEAD).astype(np.float32)
    whole = pl.BlockSpec((C, C), lambda i, *s: (0, 0))
    blocks = []
    for x in xs:
        if x.ndim == 3:
            blocks.append(pl.BlockSpec((x.shape[0], pixels, C), lambda i, *s: (0, i, 0)))
        else:
            shape = (x.shape[0], 1, x.shape[2], pixels, C)
            blocks.append(pl.BlockSpec(shape, lambda i, s: (0, s[FRAMES // 2], 0, i, 0)))
    pairs = FRAMES // 2
    return pl.pallas_call(
        functools.partial(attention_kernel, len(xs), not slots),
        out_shape=jax.ShapeDtypeStruct((pairs, 2, count, C), BF16),
        grid_spec=pltpu.PrefetchScalarGridSpec(
            num_scalar_prefetch=len(slots),
            grid=(count // pixels,),
            in_specs=blocks + [whole] * 7,
            out_specs=pl.BlockSpec((pairs, 2, pixels, C), lambda i, *s: (0, 0, i, 0)),
        ),
        compiler_params=pltpu.CompilerParams(vmem_limit_bytes=VMEM),
        cost_estimate=pl.CostEstimate(flops=cost, bytes_accessed=cost // 1000, transcendentals=0),
        name="attention",
    )(*slots, *xs, *weights, jnp.asarray(perm, BF16), jnp.asarray(perm.T, BF16), jnp.asarray(same, BF16))


def silu(v):
    return v / (1.0 + jnp.exp(-v))


EARLY = (0, 3)
LATE = (1, 2)


def hidden_row(clip_refs, proj_ref, i):
    p = jnp.concatenate([proj_ref[4 * i + j, 0] for j in range(4)], axis=0)
    return clip_refs[i // 2][0, i % 2].astype(F32) + p.astype(F32)


def put(act_ref, slot, act):
    width = act.shape[0]
    pix = lax.broadcasted_iota(jnp.int32, act.shape, 0)
    before = jnp.where(pix == 0, 0.0, pltpu.roll(act, 1, 0))
    after = jnp.where(pix == width - 1, 0.0, pltpu.roll(act, width - 1, 0))
    act_ref[slot, :, 0:C] = before.astype(BF16)
    act_ref[slot, :, C : 2 * C] = act.astype(BF16)
    act_ref[slot, :, 2 * C :] = after.astype(BF16)


def activate(hidden):
    return silu(hidden).astype(BF16).astype(F32)


def early_kernel(top_ref, bottom_ref, proj_ref, w_ref, bias_ref, part_ref, last_ref, lead_ref, act_ref):
    bias = bias_ref[...]

    def load(i):
        hidden = hidden_row((top_ref, bottom_ref), proj_ref, i)
        put(act_ref, i, activate(hidden))
        return hidden + bias

    first = load(0)
    second = load(1)
    part_ref[0, 0] = first + dot(act_ref[0], w_ref[1]) + dot(act_ref[1], w_ref[2])
    sixth = load(2)
    part_ref[0, 1] = second + dot(act_ref[0], w_ref[0]) + dot(act_ref[1], w_ref[1])
    part_ref[0, 2] = dot(act_ref[1], w_ref[0])
    seventh = load(3)
    part_ref[0, 3] = dot(act_ref[2], w_ref[2])
    part_ref[0, 4] = sixth + dot(act_ref[2], w_ref[1]) + dot(act_ref[3], w_ref[2])
    part_ref[0, 5] = seventh + dot(act_ref[2], w_ref[0]) + dot(act_ref[3], w_ref[1])
    last_ref[0, 0] = act_ref[3, :, C : 2 * C]
    lead_ref[0, 0] = act_ref[0, :, C : 2 * C]


def late_kernel(top_ref, bottom_ref, proj_ref, up_ref, down_ref, part_ref, w_ref, bias_ref, out_ref, act_ref, hid_ref):
    bias = bias_ref[...]

    def load(i):
        hidden = hidden_row((top_ref, bottom_ref), proj_ref, i)
        hid_ref[i] = hidden + bias
        put(act_ref, i, activate(hidden))

    def finish(row, acc):
        mixed = acc.astype(BF16)
        out_ref[0, 2 * row] = mixed[:, : C // 2]
        out_ref[0, 2 * row + 1] = mixed[:, C // 2 :]

    put(act_ref, 4, up_ref[0, 0].astype(F32))
    load(0)
    finish(0, part_ref[0, 0] + dot(act_ref[4], w_ref[0]))
    load(1)
    finish(1, part_ref[0, 1] + dot(act_ref[0], w_ref[2]))
    load(2)
    finish(2, part_ref[0, 2] + hid_ref[0] + dot(act_ref[0], w_ref[1]) + dot(act_ref[1], w_ref[2]))
    load(3)
    for row in (3, 4):
        acc = hid_ref[row - 2]
        for dy in range(3):
            acc = acc + dot(act_ref[row - 3 + dy], w_ref[dy])
        finish(row, acc)
    put(act_ref, 5, down_ref[0, 0].astype(F32))
    finish(5, part_ref[0, 3] + hid_ref[3] + dot(act_ref[2], w_ref[0]) + dot(act_ref[3], w_ref[1]))
    finish(6, part_ref[0, 4] + dot(act_ref[3], w_ref[0]))
    finish(7, part_ref[0, 5] + dot(act_ref[5], w_ref[2]))


def row_pair(clip, i):
    return pl.BlockSpec((1, 2) + clip.shape[2:], lambda f: (f, i, 0, 0))


def per_frame(shape):
    zeros = (0,) * (len(shape) - 1)
    return pl.BlockSpec((1,) + shape[1:], lambda f: (f,) + zeros)


def conv_specs(width, places, share):
    return (
        pl.BlockSpec((places, 1, share, C), lambda f: (0, f, 0, 0)),
        pl.BlockSpec((3, 3 * C, C), lambda f: (0, 0, 0)),
        pl.BlockSpec((1, C), lambda f: (0, 0)),
    )


def cost(frames, rows, width):
    return pl.CostEstimate(
        flops=2 * frames * rows * width * 9 * C * C,
        bytes_accessed=8 * frames * rows * width * C,
        transcendentals=frames * rows * width * C,
    )


def conv_early(clip, proj, w, bias):
    frames, rows, width, _ = clip.shape
    proj_spec, w_spec, bias_spec = conv_specs(width, proj.shape[0], proj.shape[2])
    edge = jax.ShapeDtypeStruct((frames, 1, width, C), BF16)
    outs = (jax.ShapeDtypeStruct((frames, 6, width, C), F32), edge, edge)
    return pl.pallas_call(
        early_kernel,
        out_shape=outs,
        grid=(frames,),
        in_specs=[row_pair(clip, EARLY[0]), row_pair(clip, EARLY[1]), proj_spec, w_spec, bias_spec],
        out_specs=tuple(per_frame(o.shape) for o in outs),
        scratch_shapes=[pltpu.VMEM((4, width, 3 * C), BF16)],
        compiler_params=pltpu.CompilerParams(vmem_limit_bytes=VMEM),
        cost_estimate=cost(frames, 4, width),
        name="conv_early",
    )(clip, clip, proj, w, bias)


def conv_late(clip, proj, up, down, part, w, bias):
    frames, rows, width, _ = clip.shape
    proj_spec, w_spec, bias_spec = conv_specs(width, proj.shape[0], proj.shape[2])
    out = jax.ShapeDtypeStruct((frames, 2 * rows, width, C // 2), BF16)
    return pl.pallas_call(
        late_kernel,
        out_shape=out,
        grid=(frames,),
        in_specs=[
            row_pair(clip, LATE[0]),
            row_pair(clip, LATE[1]),
            proj_spec,
            per_frame(up.shape),
            per_frame(down.shape),
            per_frame(part.shape),
            w_spec,
            bias_spec,
        ],
        out_specs=per_frame(out.shape),
        scratch_shapes=[pltpu.VMEM((6, width, 3 * C), BF16), pltpu.VMEM((4, width, C), F32)],
        compiler_params=pltpu.CompilerParams(vmem_limit_bytes=VMEM),
        cost_estimate=cost(frames, 4, width),
        name="conv_late",
    )(clip, clip, proj, up, down, part, w, bias)


def early_cut_kernel(clip_ref, out_ref):
    for f in range(out_ref.shape[2]):
        out_ref[:, :, f] = clip_ref[f]


def early_cut(clip, owners):
    frames, rows, width, _ = clip.shape
    share = 4 * width // owners
    runs = width // share
    return pl.pallas_call(
        early_cut_kernel,
        out_shape=jax.ShapeDtypeStruct((4, runs, frames, share, C), BF16),
        grid=(2,),
        in_specs=[pl.BlockSpec((frames, 2, runs, share, C), lambda i: (0, EARLY[1] * i, 0, 0, 0))],
        out_specs=pl.BlockSpec((2, runs, frames, share, C), lambda i: (i, 0, 0, 0, 0)),
        compiler_params=pltpu.CompilerParams(vmem_limit_bytes=VMEM),
        cost_estimate=pl.CostEstimate(flops=1000, bytes_accessed=1000, transcendentals=0),
        name="early_cut",
    )(clip.reshape(frames, rows, runs, share, C)).reshape(owners, frames, share, C)


def late_cut_kernel(half_ref, clip_ref, out_ref):
    for f in range(out_ref.shape[2]):
        out_ref[:, :, f] = clip_ref[f]


def late_cut(half, clip, owners):
    frames, rows, width, _ = clip.shape
    share = 4 * width // owners
    runs = width // share
    out = pl.pallas_call(
        late_cut_kernel,
        out_shape=jax.ShapeDtypeStruct((2, runs, frames, share, C), BF16),
        grid_spec=pltpu.PrefetchScalarGridSpec(
            num_scalar_prefetch=1,
            grid=(1,),
            in_specs=[pl.BlockSpec((frames, 2, runs, share, C), lambda i, s: (0, LATE[0] + s[0], 0, 0, 0))],
            out_specs=pl.BlockSpec((2, runs, frames, share, C), lambda i, s: (0, 0, 0, 0, 0)),
        ),
        compiler_params=pltpu.CompilerParams(vmem_limit_bytes=VMEM),
        cost_estimate=pl.CostEstimate(flops=1000, bytes_accessed=1000, transcendentals=0),
        name="late_cut",
    )(half, clip.reshape(frames, rows, runs, share, C))
    return out.reshape(owners // 4, 2, frames, share, C)


CHIPS = 8


def exchange(a):
    return lax.all_to_all(a, "frames", split_axis=0, concat_axis=0, tiled=True)


def to_chip(a, k):
    pairs = []
    for i in range(2 * CHIPS):
        x, y, core = i // 8, i // 2 % 4, i % 2
        pairs.append((i, ((x + core) % 2 * 4 + (y + k) % 4) * 2 + core))
    return lax.ppermute(a, "frames", pairs)


def to_sibling(a):
    return lax.ppermute(a, "frames", [(i, i ^ 1) for i in range(2 * CHIPS)])


def pick(a, i, axis=0):
    return lax.dynamic_index_in_dim(a, i, axis, keepdims=False)


def local(clip, w_query, w_key, w_value, w_out, w_conv, conv_bias):
    weights = (w_query, w_key, w_value, w_out)
    frames, rows, width, chans = clip.shape
    me = lax.axis_index("frames")
    x, y, core = me // 8, me // 2 % 4, me % 2
    other = 1 - core
    w = w_conv.reshape(3, 3 * C, C)
    bias = conv_bias.reshape(1, C)

    early, clip_late = lax.optimization_barrier((early_cut(clip, 2 * CHIPS), clip))
    early = exchange(early)
    share = early.shape[2]
    early = early.reshape(FRAMES, share, chans)

    theirs = to_sibling(late_cut((x + other).astype(jnp.int32).reshape(1) % 2, clip_late, 2 * CHIPS))
    clip_late, theirs = lax.optimization_barrier((clip_late, theirs))
    mine = late_cut((x + core).astype(jnp.int32).reshape(1) % 2, clip_late, 2 * CHIPS)
    got = []
    for k in range(4):
        to = (y + k) % 4
        got.append(to_chip(jnp.stack([pick(mine, to), pick(theirs, to)]), k))

    proj = attention(None, [early], weights, 64, 1000)
    proj_early = exchange(proj)
    _, *got = lax.optimization_barrier((proj, *got))

    give = jnp.stack([pick(g, other, 1) for g in got]).reshape(FRAMES // 2, share, chans)
    theirs = to_sibling(give)
    slots = []
    for c in (core, other):
        for k in range(4):
            for s in range(2):
                slots.append(((x + c) % 2 * 4 + (y + 4 - k) % 4) * 2 + (c + s) % 2)
    slots = jnp.stack(slots + [core]).astype(jnp.int32)
    proj_late = exchange(attention(slots, [*got, theirs], weights, 64, 5 * 10**9))

    part, last, lead = conv_early(clip, proj_early, w, bias)
    size = lax.axis_size("rows")
    up = lax.ppermute(last, "rows", [(i, i + 1) for i in range(size - 1)])
    down = lax.ppermute(lead, "rows", [(i + 1, i) for i in range(size - 1)])
    return conv_late(clip, proj_late, up, down, part, w, bias)


def solution(mesh):
    placed = (P("frames", "rows", None, None), P(), P(), P(), P(), P(), P())
    return jax.shard_map(
        local,
        mesh=mesh,
        in_specs=placed,
        out_specs=P("frames", "rows", None, None),
        check_vma=False,
    )
```

```python
import functools

import jax
import jax.numpy as jnp
import numpy as np
from jax import lax
from jax.experimental import pallas as pl
from jax.experimental.pallas import tpu as pltpu
from jax.sharding import PartitionSpec as P

HEADS = 8
HEAD = 32
FRAMES = 32
C = 256
GROUP = 8
VMEM = 63 * 2**20
F32 = jnp.float32
BF16 = jnp.bfloat16


def dot(a, b):
    return jnp.dot(a, b, preferred_element_type=F32)


def dot_nt(a, b):
    return lax.dot_general(a, b, (((1,), (1,)), ((), ())), preferred_element_type=F32)


def group_max(s):
    t = s.T
    rows = t.shape[1]
    m = jnp.max(t.reshape(HEADS, HEAD, rows), axis=1, keepdims=True)
    return jnp.broadcast_to(m, (HEADS, HEAD, rows)).reshape(C, rows).T


def attention_kernel(parts_in, ordered, *refs):
    slots_ref, refs = (range(FRAMES // 2), refs) if ordered else (refs[0], refs[1:])
    x_refs = refs[:parts_in]
    wq_ref, wk_ref, wv_ref, wo_ref, perm_ref, back_ref, same_ref = refs[parts_in : parts_in + 7]
    out_ref = refs[-1]
    pixels = x_refs[0].shape[-2]
    x = jnp.concatenate([r[...].reshape(-1, pixels, C) for r in x_refs], axis=0).astype(F32)
    mean = jnp.mean(x, axis=-1, keepdims=True)
    centred = x - mean
    var = jnp.mean(centred * centred, axis=-1, keepdims=True)
    normed = centred * lax.rsqrt(var + 1e-6)
    rows = GROUP * FRAMES
    parts = []
    for j in range(pixels // GROUP):
        part = normed[:, j * GROUP : (j + 1) * GROUP].reshape(rows, C).astype(BF16)
        parts.append(dot(perm_ref[...], part).astype(BF16))
    xp = jnp.concatenate(parts, axis=0)
    q = dot(xp, wq_ref[...]).astype(BF16)
    k = dot(xp, wk_ref[...]).astype(BF16)
    v = dot(xp, wv_ref[...]).astype(BF16)
    same = same_ref[...]
    scores = []
    for p in range(pixels):
        at = slice(p * FRAMES, (p + 1) * FRAMES)
        scores.append(dot_nt(q[at], jnp.concatenate([k[at]] * HEADS, axis=0) * same))
    s = jnp.concatenate(scores, axis=0)
    factor = np.float32(np.log2(np.e) / np.sqrt(HEAD))
    e = jnp.exp2((s - group_max(s)) * factor).astype(BF16)
    total = dot(e, same)
    sums = []
    for p in range(pixels):
        at = slice(p * FRAMES, (p + 1) * FRAMES)
        sums.append(dot(e[at], jnp.concatenate([v[at]] * HEADS, axis=0) * same))
    attended = (jnp.concatenate(sums, axis=0) / total).astype(BF16)
    projected = dot(attended, wo_ref[...]).astype(BF16)
    for j in range(pixels // GROUP):
        part = dot(back_ref[...], projected[j * rows : (j + 1) * rows])
        parts[j] = part.reshape(FRAMES, GROUP, C)
    out = jnp.concatenate(parts, axis=1).astype(BF16)
    for i in range(FRAMES // 2):
        out_ref[slots_ref[i]] = out[2 * i : 2 * i + 2]


def attention(slots, xs, weights, pixels, cost):
    slots = [] if slots is None else [slots]
    count = xs[0].shape[-2]
    row = np.arange(GROUP * FRAMES)
    source = (row % FRAMES) * GROUP + row // FRAMES
    perm = (source[:, None] == row[None, :]).astype(np.float32)
    same = (row[:, None] // HEAD == row[None, :] // HEAD).astype(np.float32)
    whole = pl.BlockSpec((C, C), lambda i, *s: (0, 0))
    blocks = []
    for x in xs:
        if x.ndim == 3:
            blocks.append(pl.BlockSpec((x.shape[0], pixels, C), lambda i, *s: (0, i, 0)))
        else:
            shape = (x.shape[0], 1, x.shape[2], pixels, C)
            blocks.append(pl.BlockSpec(shape, lambda i, s: (0, s[FRAMES // 2], 0, i, 0)))
    pairs = FRAMES // 2
    return pl.pallas_call(
        functools.partial(attention_kernel, len(xs), not slots),
        out_shape=jax.ShapeDtypeStruct((pairs, 2, count, C), BF16),
        grid_spec=pltpu.PrefetchScalarGridSpec(
            num_scalar_prefetch=len(slots),
            grid=(count // pixels,),
            in_specs=blocks + [whole] * 7,
            out_specs=pl.BlockSpec((pairs, 2, pixels, C), lambda i, *s: (0, 0, i, 0)),
        ),
        compiler_params=pltpu.CompilerParams(vmem_limit_bytes=VMEM),
        cost_estimate=pl.CostEstimate(flops=cost, bytes_accessed=cost // 1000, transcendentals=0),
        name="attention",
    )(*slots, *xs, *weights, jnp.asarray(perm, BF16), jnp.asarray(perm.T, BF16), jnp.asarray(same, BF16))


def silu(v):
    return v / (1.0 + jnp.exp(-v))


EARLY = (0, 3)
LATE = (1, 2)


def hidden_row(clip_refs, proj_ref, i):
    p = jnp.concatenate([proj_ref[4 * i + j, 0] for j in range(4)], axis=0)
    return clip_refs[i // 2][0, i % 2].astype(F32) + p.astype(F32)


def put(act_ref, slot, act):
    width = act.shape[0]
    pix = lax.broadcasted_iota(jnp.int32, act.shape, 0)
    before = jnp.where(pix == 0, 0.0, pltpu.roll(act, 1, 0))
    after = jnp.where(pix == width - 1, 0.0, pltpu.roll(act, width - 1, 0))
    act_ref[slot, :, 0:C] = before.astype(BF16)
    act_ref[slot, :, C : 2 * C] = act.astype(BF16)
    act_ref[slot, :, 2 * C :] = after.astype(BF16)


def activate(hidden):
    return silu(hidden).astype(BF16).astype(F32)


def early_kernel(top_ref, bottom_ref, proj_ref, w_ref, bias_ref, part_ref, last_ref, lead_ref, act_ref):
    bias = bias_ref[...]

    def load(i):
        hidden = hidden_row((top_ref, bottom_ref), proj_ref, i)
        put(act_ref, i, activate(hidden))
        return hidden + bias

    first = load(0)
    second = load(1)
    part_ref[0, 0] = first + dot(act_ref[0], w_ref[1]) + dot(act_ref[1], w_ref[2])
    sixth = load(2)
    part_ref[0, 1] = second + dot(act_ref[0], w_ref[0]) + dot(act_ref[1], w_ref[1])
    part_ref[0, 2] = dot(act_ref[1], w_ref[0])
    seventh = load(3)
    part_ref[0, 3] = dot(act_ref[2], w_ref[2])
    part_ref[0, 4] = sixth + dot(act_ref[2], w_ref[1]) + dot(act_ref[3], w_ref[2])
    part_ref[0, 5] = seventh + dot(act_ref[2], w_ref[0]) + dot(act_ref[3], w_ref[1])
    last_ref[0, 0] = act_ref[3, :, C : 2 * C]
    lead_ref[0, 0] = act_ref[0, :, C : 2 * C]


def late_kernel(top_ref, bottom_ref, proj_ref, up_ref, down_ref, part_ref, w_ref, bias_ref, out_ref, act_ref, hid_ref):
    bias = bias_ref[...]

    def load(i):
        hidden = hidden_row((top_ref, bottom_ref), proj_ref, i)
        hid_ref[i] = hidden + bias
        put(act_ref, i, activate(hidden))

    def finish(row, acc):
        mixed = acc.astype(BF16)
        out_ref[0, 2 * row] = mixed[:, : C // 2]
        out_ref[0, 2 * row + 1] = mixed[:, C // 2 :]

    put(act_ref, 4, up_ref[0, 0].astype(F32))
    load(0)
    finish(0, part_ref[0, 0] + dot(act_ref[4], w_ref[0]))
    load(1)
    finish(1, part_ref[0, 1] + dot(act_ref[0], w_ref[2]))
    load(2)
    finish(2, part_ref[0, 2] + hid_ref[0] + dot(act_ref[0], w_ref[1]) + dot(act_ref[1], w_ref[2]))
    load(3)
    for row in (3, 4):
        acc = hid_ref[row - 2]
        for dy in range(3):
            acc = acc + dot(act_ref[row - 3 + dy], w_ref[dy])
        finish(row, acc)
    put(act_ref, 5, down_ref[0, 0].astype(F32))
    finish(5, part_ref[0, 3] + hid_ref[3] + dot(act_ref[2], w_ref[0]) + dot(act_ref[3], w_ref[1]))
    finish(6, part_ref[0, 4] + dot(act_ref[3], w_ref[0]))
    finish(7, part_ref[0, 5] + dot(act_ref[5], w_ref[2]))


def row_pair(clip, i):
    return pl.BlockSpec((1, 2) + clip.shape[2:], lambda f: (f, i, 0, 0))


def per_frame(shape):
    zeros = (0,) * (len(shape) - 1)
    return pl.BlockSpec((1,) + shape[1:], lambda f: (f,) + zeros)


def conv_specs(width, places, share):
    return (
        pl.BlockSpec((places, 1, share, C), lambda f: (0, f, 0, 0)),
        pl.BlockSpec((3, 3 * C, C), lambda f: (0, 0, 0)),
        pl.BlockSpec((1, C), lambda f: (0, 0)),
    )


def cost(frames, rows, width):
    return pl.CostEstimate(
        flops=2 * frames * rows * width * 9 * C * C,
        bytes_accessed=8 * frames * rows * width * C,
        transcendentals=frames * rows * width * C,
    )


def conv_early(clip, proj, w, bias):
    frames, rows, width, _ = clip.shape
    proj_spec, w_spec, bias_spec = conv_specs(width, proj.shape[0], proj.shape[2])
    edge = jax.ShapeDtypeStruct((frames, 1, width, C), BF16)
    outs = (jax.ShapeDtypeStruct((frames, 6, width, C), F32), edge, edge)
    return pl.pallas_call(
        early_kernel,
        out_shape=outs,
        grid=(frames,),
        in_specs=[row_pair(clip, EARLY[0]), row_pair(clip, EARLY[1]), proj_spec, w_spec, bias_spec],
        out_specs=tuple(per_frame(o.shape) for o in outs),
        scratch_shapes=[pltpu.VMEM((4, width, 3 * C), BF16)],
        compiler_params=pltpu.CompilerParams(vmem_limit_bytes=VMEM),
        cost_estimate=cost(frames, 4, width),
        name="conv_early",
    )(clip, clip, proj, w, bias)


def conv_late(clip, proj, up, down, part, w, bias):
    frames, rows, width, _ = clip.shape
    proj_spec, w_spec, bias_spec = conv_specs(width, proj.shape[0], proj.shape[2])
    out = jax.ShapeDtypeStruct((frames, 2 * rows, width, C // 2), BF16)
    return pl.pallas_call(
        late_kernel,
        out_shape=out,
        grid=(frames,),
        in_specs=[
            row_pair(clip, LATE[0]),
            row_pair(clip, LATE[1]),
            proj_spec,
            per_frame(up.shape),
            per_frame(down.shape),
            per_frame(part.shape),
            w_spec,
            bias_spec,
        ],
        out_specs=per_frame(out.shape),
        scratch_shapes=[pltpu.VMEM((6, width, 3 * C), BF16), pltpu.VMEM((4, width, C), F32)],
        compiler_params=pltpu.CompilerParams(vmem_limit_bytes=VMEM),
        cost_estimate=cost(frames, 4, width),
        name="conv_late",
    )(clip, clip, proj, up, down, part, w, bias)


def early_cut_kernel(clip_ref, out_ref):
    for f in range(out_ref.shape[2]):
        out_ref[:, :, f] = clip_ref[f]


def early_cut(clip, owners):
    frames, rows, width, _ = clip.shape
    share = 4 * width // owners
    runs = width // share
    return pl.pallas_call(
        early_cut_kernel,
        out_shape=jax.ShapeDtypeStruct((4, runs, frames, share, C), BF16),
        grid=(2,),
        in_specs=[pl.BlockSpec((frames, 2, runs, share, C), lambda i: (0, EARLY[1] * i, 0, 0, 0))],
        out_specs=pl.BlockSpec((2, runs, frames, share, C), lambda i: (i, 0, 0, 0, 0)),
        compiler_params=pltpu.CompilerParams(vmem_limit_bytes=VMEM),
        cost_estimate=pl.CostEstimate(flops=1000, bytes_accessed=1000, transcendentals=0),
        name="early_cut",
    )(clip.reshape(frames, rows, runs, share, C)).reshape(owners, frames, share, C)


CHIPS = 8


def exchange(a):
    return lax.all_to_all(a, "frames", split_axis=0, concat_axis=0, tiled=True)


def to_chip(a, k):
    pairs = []
    for i in range(2 * CHIPS):
        x, y, core = i // 8, i // 2 % 4, i % 2
        pairs.append((i, ((x + core) % 2 * 4 + (y + k) % 4) * 2 + core))
    return lax.ppermute(a, "frames", pairs)


def to_sibling(a):
    return lax.ppermute(a, "frames", [(i, i ^ 1) for i in range(2 * CHIPS)])


def pick(a, i, axis=0):
    return lax.dynamic_index_in_dim(a, i, axis, keepdims=False)


def local(clip, w_query, w_key, w_value, w_out, w_conv, conv_bias):
    weights = (w_query, w_key, w_value, w_out)
    frames, rows, width, chans = clip.shape
    me = lax.axis_index("frames")
    x, y, core = me // 8, me // 2 % 4, me % 2
    other = 1 - core
    w = w_conv.reshape(3, 3 * C, C)
    bias = conv_bias.reshape(1, C)

    early, clip_late = lax.optimization_barrier((early_cut(clip, 2 * CHIPS), clip))
    early = exchange(early)
    share = early.shape[2]
    early = early.reshape(FRAMES, share, chans)

    clip_late = clip_late.reshape(frames, rows, 4, share, chans)

    def rows_for(half):
        return lax.dynamic_slice_in_dim(clip_late, 2 * LATE[0] + 2 * half, 2, 1)

    def pixels_for(source, to):
        run = lax.dynamic_slice(source, (0, to // 2, to % 2 * 2, 0, 0), (frames, 1, 2, share, chans))
        return run[:, 0].transpose(1, 0, 2, 3)

    theirs = to_sibling(rows_for((x + other) % 2))
    mine = rows_for((x + core) % 2)
    got = []
    for k in range(4):
        to = (y + k) % 4
        got.append(to_chip(jnp.stack([pixels_for(mine, to), pixels_for(theirs, to)]), k))

    proj = attention(None, [early], weights, 64, 1000)
    proj_early = exchange(proj)
    _, *got = lax.optimization_barrier((proj, *got))

    give = jnp.stack([pick(g, other, 1) for g in got]).reshape(FRAMES // 2, share, chans)
    theirs = to_sibling(give)
    slots = []
    for c in (core, other):
        for k in range(4):
            for s in range(2):
                slots.append(((x + c) % 2 * 4 + (y + 4 - k) % 4) * 2 + (c + s) % 2)
    slots = jnp.stack(slots + [core]).astype(jnp.int32)
    proj_late = exchange(attention(slots, [*got, theirs], weights, 64, 5 * 10**9))

    part, last, lead = conv_early(clip, proj_early, w, bias)
    size = lax.axis_size("rows")
    up = lax.ppermute(last, "rows", [(i, i + 1) for i in range(size - 1)])
    down = lax.ppermute(lead, "rows", [(i + 1, i) for i in range(size - 1)])
    return conv_late(clip, proj_late, up, down, part, w, bias)


def solution(mesh):
    placed = (P("frames", "rows", None, None), P(), P(), P(), P(), P(), P())
    return jax.shard_map(
        local,
        mesh=mesh,
        in_specs=placed,
        out_specs=P("frames", "rows", None, None),
        check_vma=False,
    )
```
